32 devices in a mesh: area: 8 (over z, x), col: 4 (over y, core).
Axes of the slice: x: 2, y: 2, z: 4, core: 2. Of those that a mesh axis runs over, the one named last changes fastest.
Arguments:
- initial_state: float32 [256, 128, 128], P(('area', 'col')), may hold values from -6 to 6
- past_rates: bfloat16 [2, 256, 128, 128], P(None, ('area', 'col')), may hold values from 0 to 2
- stimulus: bfloat16 [256, 128, 128], P(('area', 'col')), may hold values from -6 to 6
- leak_rate: float32 [256, 128], P(('area', 'col')), may hold values from 0.05 to 0.5
- local_weight: bfloat16 [256, 12, 128, 128], P(('area', 'col')), may hold values from -0.125 to 0.125
- far_weight: bfloat16 [256, 8, 128, 128], P(('area', 'col')), may hold values from -0.125 to 0.125
- local_index: int32 [256, 12], P(('area', 'col')), may hold values from 0 to 31, all different within a row
- area_sizes: int32 [4], replicated, may hold values from 1 to 3, as said below
- far_area: int32 [256, 8], replicated, may hold values from 0 to 3, as said below
- far_offset: int32 [256, 8], replicated, may hold values from 0 to 95, as said below
Outputs:
- final_state: float32 [256, 128, 128], P(('area', 'col'))
The draws below stay inside these ranges and needn't reach their ends.
Inputs may be any that keep to these rules, and one draw needn't show every extreme that they name: `area_sizes`: Areas' section counts sum to 8; some area has exactly 3 sections. `far_area`: the source area of a far link differs from the area that holds its block row. In each aligned group of 8 block rows, at most 16 far links read blocks of one section (blocks s * 32 to s * 32 + 31), and exactly 16 read some section. `far_offset`: each offset lies below its source area's sections times 32.
All inputs are finite; a program needn't handle non-finite values.
Results may differ from the reference program's by a relative error of at most 0.0009.
Values may be sent and summed in bfloat16 or wider, within the bound.
A program may use at most 128 MiB of HBM per device.

```python
import math
import jax
import jax.numpy as jnp
from jax import lax

BLOCK = 128
TRIALS = 128
BLK_DEV = 8
LOCAL = 12
FAR = 8
AREAS = 4
STEPS = 4
DELAY = 2
SEC_BLK = 32
NB = 256
MOST_AREA = 3
CAP = 16
N_AREA = 8
N_COL = 4


def link_tables(key):
    base = jax.random.fold_in(key, 7)
    key_big, key_spread, key_device = jax.random.split(base, 3)
    extra_cap = max(MOST_AREA - 1, 1)
    big_area = jax.random.randint(key_big, (), 0, AREAS)
    slot_area = jnp.arange(AREAS * extra_cap, dtype=jnp.int32) // extra_cap
    priority = jax.random.permutation(key_spread, AREAS * extra_cap).astype(jnp.int32)
    priority = jnp.where(slot_area == big_area, AREAS * extra_cap + priority, priority)
    slot_rank = jnp.argsort(jnp.argsort(priority))
    spread_total = N_AREA - AREAS - (MOST_AREA - 1)
    chosen = (slot_rank < spread_total).astype(jnp.int32)
    area_ids = jnp.arange(AREAS, dtype=jnp.int32)
    counts = jnp.sum(chosen[None, :] * (slot_area[None, :] == area_ids[:, None]).astype(jnp.int32), axis=1)
    sizes = (1 + counts + (MOST_AREA - 1) * (area_ids == big_area).astype(jnp.int32)).astype(jnp.int32)
    starts = jnp.cumsum(sizes) - sizes
    section_ids = jnp.arange(N_AREA, dtype=jnp.int32)
    area_of_section = (jnp.sum((starts[None, :] <= section_ids[:, None]).astype(jnp.int32), axis=1) - 1).astype(jnp.int32)
    device_count = N_AREA * N_COL
    link_count = BLK_DEV * FAR
    device_ids = jnp.arange(device_count, dtype=jnp.int32)
    own_area = area_of_section[device_ids // N_COL]

    def one_device(device_key, home_area):
        key_forced, key_order, key_shuffle, key_within = jax.random.split(device_key, 4)
        slot_section = jnp.arange(N_AREA * CAP, dtype=jnp.int32) // CAP
        eligible = area_of_section[slot_section] != home_area
        section_ok = area_of_section != home_area
        scores = jax.random.randint(key_forced, (N_AREA,), 0, 1 << 20) * N_AREA + section_ids
        forced = jnp.argmax(jnp.where(section_ok, scores, -1))
        order_perm = jax.random.permutation(key_order, N_AREA * CAP).astype(jnp.int32)
        ranking = jnp.where(slot_section == forced, order_perm - 2 * N_AREA * CAP, order_perm)
        ranking = jnp.where(eligible, ranking, order_perm + 2 * N_AREA * CAP)
        picked = jnp.argsort(ranking)[:link_count]
        shuffle = jax.random.permutation(key_shuffle, link_count)
        slots = picked[shuffle]
        section_pick = (slots // CAP).astype(jnp.int32)
        within = jax.random.randint(key_within, (link_count,), 0, SEC_BLK)
        return (section_pick, within)
    device_keys = jax.vmap(lambda number: jax.random.fold_in(key_device, number))(device_ids)
    section_pick, within = jax.vmap(one_device)(device_keys, own_area)
    source_area = area_of_section[section_pick]
    offsets = (section_pick - starts[source_area]) * SEC_BLK + within
    return (sizes, source_area.reshape(NB, FAR).astype(jnp.int32), offsets.reshape(NB, FAR).astype(jnp.int32))


def draw_area_sizes(key, part):
    return link_tables(key)[0]


def draw_far_area(key, part):
    return link_tables(key)[1]


def draw_far_offset(key, part):
    return link_tables(key)[2]


def shard_levels(stream_key, dims, cuts, smallest, high):
    level, own = 1.0, jax.random.fold_in(stream_key, 6)
    for dim, shards_of in cuts:
        heights = jnp.exp(jax.random.uniform(jax.random.fold_in(own, dim), (shards_of,), jnp.float32, smallest / len(cuts), high / len(cuts)))
        level = level * jnp.repeat(heights, dims[dim] // shards_of).reshape([-1 if axis == dim else 1 for axis in range(len(dims))])
    return level


def distinct(stream_key, rows, amount, top, lift):
    sequence = jax.random.permutation(jax.random.fold_in(stream_key, 1), amount)
    boost = sequence
    for power in range(3):
        boost = boost * boost // amount
    boost = boost * lift // amount
    tickets = jax.random.randint(jax.random.fold_in(stream_key, 2), (rows, amount), 0, 4096) + boost
    holders = jax.random.permutation(jax.random.fold_in(stream_key, 3), rows)[jnp.arange(amount) % rows]
    tickets = jnp.where(jnp.arange(rows)[:, None] == holders[None, :], 1 << 14, tickets)
    merit = tickets * amount + jnp.arange(amount)
    return lax.top_k(merit.astype(jnp.int32), top)[1].astype(jnp.int32)


def scatter_about(stream_key, dims, deviation, most, cuts=(), kind=jnp.bfloat16):
    entries = jax.random.normal(stream_key, dims, jnp.float32) * deviation
    if len(cuts) > 0:
        entries = shard_levels(stream_key, dims, cuts, -0.22, 0.18) * entries
    return jnp.clip(entries, min=-most, max=most).astype(kind)


def setup_inputs(seed: int = 0) -> dict:
    streams_of = jax.random.split(jax.random.key(seed), 11)
    initial_state = scatter_about(streams_of[0], (NB, TRIALS, BLOCK), 1.0, 6.0, ((0, 32),), jnp.float32)
    past_rates = jnp.clip(2.0 * jax.random.uniform(streams_of[1], (DELAY, NB, TRIALS, BLOCK), jnp.float32) ** shard_levels(streams_of[1], (DELAY, NB, TRIALS, BLOCK), ((1, 32),), -0.2, 0.2), 0.0, 2.0).astype(jnp.bfloat16)
    stimulus = scatter_about(streams_of[2], (NB, TRIALS, BLOCK), 1.0, 6.0, ((0, 32),))
    leak_rate = jnp.clip(jnp.exp(math.log(0.5) - 2.3025851 * jax.random.uniform(streams_of[3], (NB, BLOCK), jnp.float32) ** shard_levels(streams_of[3], (NB, BLOCK), ((0, 32),), -0.2, 0.2)), 0.05, 0.5)
    local_weight = scatter_about(streams_of[4], (NB, LOCAL, BLOCK, BLOCK), ((LOCAL + FAR) * BLOCK) ** -0.5, 0.125, ((0, 32),))
    far_weight = scatter_about(streams_of[5], (NB, FAR, BLOCK, BLOCK), ((LOCAL + FAR) * BLOCK) ** -0.5, 0.125, ((0, 32),))
    local_index = distinct(streams_of[6], NB, SEC_BLK, LOCAL, 6144)
    area_sizes = draw_area_sizes(jax.random.fold_in(streams_of[10], 71), 0)
    far_area = draw_far_area(jax.random.fold_in(streams_of[10], 71), 0)
    far_offset = draw_far_offset(jax.random.fold_in(streams_of[10], 71), 0)
    return dict(initial_state=initial_state, past_rates=past_rates, stimulus=stimulus, leak_rate=leak_rate, local_weight=local_weight, far_weight=far_weight, local_index=local_index, area_sizes=area_sizes, far_area=far_area, far_offset=far_offset)


def reference(initial_state, past_rates, stimulus, leak_rate, local_weight, far_weight, local_index, area_sizes, far_area, far_offset):
    area_first = (jnp.cumsum(area_sizes) - area_sizes).astype(jnp.int32)
    area_len = area_sizes[far_area].astype(jnp.int32)
    first_sel = area_first[far_area].astype(jnp.int32)
    far_block = (first_sel * SEC_BLK + far_offset % (area_len * SEC_BLK)).astype(jnp.int32)
    row_ids = jnp.arange(NB, dtype=jnp.int32)
    local_block = (((row_ids // SEC_BLK) * SEC_BLK)[:, None] + local_index).astype(jnp.int32)

    def currents(rate_now, rate_late):
        def per_group(inputs):
            near_ids, far_ids, near_weight, distant_weight = inputs
            lateral = jnp.einsum("rktb,rkob->rto", rate_now[near_ids].astype(jnp.float32), near_weight.astype(jnp.float32), precision=lax.Precision.HIGHEST)
            distant = jnp.einsum("rktb,rkob->rto", rate_late[far_ids].astype(jnp.float32), distant_weight.astype(jnp.float32), precision=lax.Precision.HIGHEST)
            return lateral, distant

        lateral, distant = lax.map(per_group, (
            local_block.reshape(N_AREA, SEC_BLK, LOCAL),
            far_block.reshape(N_AREA, SEC_BLK, FAR),
            local_weight.reshape(N_AREA, SEC_BLK, LOCAL, BLOCK, BLOCK),
            far_weight.reshape(N_AREA, SEC_BLK, FAR, BLOCK, BLOCK)))
        return lateral.reshape(NB, TRIALS, BLOCK), distant.reshape(NB, TRIALS, BLOCK)

    membrane = initial_state
    history = [past_rates[index] for index in range(DELAY)]
    history.append(jax.nn.softplus(membrane).astype(jnp.bfloat16))
    drive_term = stimulus.astype(jnp.float32)
    for step_idx in range(STEPS):
        lateral, distant = currents(history[step_idx + DELAY], history[step_idx])
        membrane = membrane + leak_rate[:, None, :] * (-membrane + lateral + distant + drive_term)
        if step_idx + 1 < STEPS:
            history.append(jax.nn.softplus(membrane).astype(jnp.bfloat16))
    return membrane
```

```python
import functools

import jax
import jax.numpy as jnp
from jax import lax
from jax.sharding import PartitionSpec as P

from jax.experimental import pallas as pl
from jax.experimental.pallas import tpu as pltpu

STEPS = 4
CORES = 2
PLANE = 2
VMEM_GRANT = 60 * 1024 * 1024


def shards_exchange(
    initial_state,
    past_rates,
    stimulus,
    leak_rate,
    local_weight,
    far_weight,
    local_index,
    area_sizes,
    far_area,
    far_offset,
):
    area_count = lax.axis_size("area")
    col_count = lax.axis_size("col")
    my_area = lax.axis_index("area")
    my_col = lax.axis_index("col")
    row_count = initial_state.shape[0]
    trial_count = initial_state.shape[1]
    block_len = initial_state.shape[2]
    link_count = row_count * far_weight.shape[1]
    slot_count = 2 * link_count // area_count
    section_len = row_count * col_count
    delay_len = past_rates.shape[0]
    area_ids = jnp.arange(area_sizes.shape[0], dtype=jnp.int32)
    starts = jnp.cumsum(area_sizes) - area_sizes
    match_area = far_area[..., None] == area_ids
    area_len = jnp.sum(jnp.where(match_area, area_sizes, 0), axis=-1)
    area_first = jnp.sum(jnp.where(match_area, starts, 0), axis=-1)
    far_block = area_first * section_len + far_offset % (area_len * section_len)
    by_device = far_block.reshape(area_count, col_count, link_count)
    same_col = lax.dynamic_index_in_dim(by_device, my_col, axis=1, keepdims=False)
    section_of = same_col // section_len
    placing = same_col % section_len
    earlier = jnp.tril(jnp.ones((link_count, link_count), jnp.bool_), -1)
    order_rank = jnp.sum(
        (section_of[:, :, None] == section_of[:, None, :]) & earlier[None], axis=-1
    )
    slot_ids = jnp.arange(slot_count, dtype=order_rank.dtype)
    wanted = (section_of[:, None, :] == my_area) & (
        order_rank[:, None, :] == slot_ids[None, :, None]
    )
    slot_place = jnp.sum(jnp.where(wanted, placing[:, None, :], 0), axis=-1).reshape(-1)
    slot_used = jnp.any(wanted, axis=-1).reshape(-1)
    own_section = lax.dynamic_index_in_dim(section_of, my_area, axis=0, keepdims=False)
    own_rank = lax.dynamic_index_in_dim(order_rank, my_area, axis=0, keepdims=False)
    arrival = own_section * slot_count + own_rank
    leak_gain = leak_rate[:, None, :]
    drive_term = stimulus.astype(jnp.float32)
    membrane = initial_state
    rate_now = jax.nn.softplus(membrane).astype(jnp.bfloat16)
    sections = []
    for step_idx in range(STEPS):
        section = lax.all_gather(rate_now, "col", axis=0, tiled=True)
        sections.append(section)
        if step_idx < delay_len:
            source = lax.all_gather(past_rates[step_idx], "col", axis=0, tiled=True)
        else:
            source = sections[step_idx - delay_len]
        frames = source[None]
        picked = frames[:, slot_place]
        arrived = lax.all_to_all(
            jnp.where(slot_used[None, :, None, None], picked, jnp.zeros((), frames.dtype)),
            "area",
            split_axis=1,
            concat_axis=1,
            tiled=True,
        )[0]
        lateral = jnp.einsum(
            "rktb,rkob->rto", section[local_index], local_weight, preferred_element_type=jnp.float32
        )
        distant = jnp.einsum(
            "rktb,rkob->rto",
            arrived[arrival].reshape(row_count, -1, trial_count, block_len),
            far_weight,
            preferred_element_type=jnp.float32,
        )
        membrane = membrane + leak_gain * (-membrane + lateral + distant + drive_term)
        if step_idx + 1 < STEPS:
            rate_now = jax.nn.softplus(membrane).astype(jnp.bfloat16)
    return membrane


def softplus(values):
    return jnp.maximum(values, 0.0) + jnp.log1p(jnp.exp(-jnp.abs(values)))


def kernel(
    dims,
    far_idx,
    local_idx,
    initial,
    stimulus,
    leak,
    past,
    local_weight,
    far_weight,
    out,
    *scratch,
):
    depth_len, rows = dims
    delay_len = past.shape[0]
    frame_count = STEPS
    far_frames = scratch[:frame_count]
    near_frames = scratch[frame_count : 2 * frame_count + delay_len]
    near_weight, distant_weight, load_sem, send_sem, recv_sem = scratch[2 * frame_count + delay_len :]
    my_area = lax.axis_index("area")
    my_col = lax.axis_index("col")
    my_depth, my_x = my_area // PLANE, my_area % PLANE
    my_y, my_core = my_col // CORES, my_col % CORES
    other_x, other_y, other_core = 1 - my_x, 1 - my_y, 1 - my_core
    col_count = lax.axis_size("col")
    half = rows // 2

    def area_at(depth_back, x_pos):
        return lax.rem(my_depth - depth_back + depth_len, depth_len) * PLANE + x_pos

    to_x = {"area": my_depth * PLANE + other_x, "col": my_col}
    to_y = {"area": my_area, "col": other_y * CORES + my_core}
    to_core = {"area": my_area, "col": my_y * CORES + other_core}

    def to_depth(step):
        return {"area": lax.rem(my_depth + step, depth_len) * PLANE + my_x, "col": my_col}

    partners = [to_depth(step) for step in range(1, depth_len)] + [to_x, to_y, to_core]

    loads = [
        pltpu.make_async_copy(
            past.at[index], near_frames[index].at[pl.ds(my_col * rows, rows)], load_sem.at[index]
        )
        for index in range(delay_len)
    ]
    loads.append(pltpu.make_async_copy(local_weight, near_weight, load_sem.at[delay_len]))
    loads.append(pltpu.make_async_copy(far_weight, distant_weight, load_sem.at[delay_len + 1]))
    for load in loads:
        load.start()

    barrier = pltpu.get_barrier_semaphore()
    for partner in partners:
        pl.semaphore_signal(barrier, inc=1, device_id=partner, device_id_type=pl.DeviceIdType.MESH)

    def prepare(row, carry):
        state = initial[row]
        out[row] = state
        near_frames[delay_len][my_col * rows + row] = softplus(state).astype(jnp.bfloat16)
        return carry

    lax.fori_loop(0, rows, prepare, 0)
    pl.semaphore_wait(barrier, len(partners))
    for load in loads[:delay_len]:
        load.wait()

    started = {}
    numbers = {}

    def near_view(frame, y_pos, core, first=0, count=None):
        start = (y_pos * CORES + core) * rows + first
        return near_frames[frame].at[pl.ds(start, rows if count is None else count)]

    def far_view(frame, area, y_pos, core, first=0, count=None):
        start = (area * col_count + y_pos * CORES + core) * rows + first
        return far_frames[frame].at[pl.ds(start, rows if count is None else count)]

    def send(key, source, target, device):
        number = numbers.setdefault(key, len(numbers))
        copy = pltpu.make_async_remote_copy(
            src_ref=source,
            dst_ref=target,
            send_sem=send_sem.at[number],
            recv_sem=recv_sem.at[number],
            device_id=device,
            device_id_type=pl.DeviceIdType.MESH,
        )
        copy.start()
        started[key] = copy

    def arrived(key):
        started[key].wait_recv()

    def own_depth(frame):
        mine = near_view(frame, my_y, my_core)
        for step in range(1, depth_len):
            send(("z", frame, step), mine, far_view(frame, my_area, my_y, my_core), to_depth(step))

    def own_x(frame):
        mine = near_view(frame, my_y, my_core)
        send(("x", frame, 0), mine, far_view(frame, my_area, my_y, my_core), to_x)

    def own_section(frame):
        if frame < delay_len:
            part = near_view(frame, my_y, my_core, half, rows - half)
            send(("y", frame, 0), part, part, to_y)
        else:
            mine = near_view(frame, my_y, my_core)
            send(("y", frame, 0), mine, mine, to_y)
            send(("c", frame), mine, mine, to_core)

    def column(frame):
        for step in range(1, depth_len):
            arrived(("z", frame, step))
            view = far_view(frame, area_at(step, my_x), my_y, my_core)
            send(("x", frame, step), view, view, to_x)
            send(("y", frame, step), view, view, to_y)
            send(("cz", frame, step), view, view, to_core)

    def section_arrival(frame):
        arrived(("y", frame, 0))
        view = near_view(frame, other_y, my_core)
        send(("cy", frame, 0), view, view, to_core)

    def section_ready(frame):
        arrived(("c", frame))
        arrived(("cy", frame, 0))

    def relay(frame):
        for step in range(depth_len):
            arrived(("x", frame, step))
            area = area_at(step, other_x)
            part = far_view(frame, area, my_y, my_core, 0, half)
            send(("dy", frame, step), part, part, to_y)
            view = far_view(frame, area, my_y, my_core)
            send(("cx", frame, step), view, view, to_core)
            area = area_at(step, my_x)
            if step == 0:
                if frame < delay_len:
                    arrived(("y", frame, 0))
                part = near_view(frame, other_y, my_core, half, rows - half)
                send(
                    ("dx", frame, step),
                    part,
                    far_view(frame, area, other_y, my_core, half, rows - half),
                    to_x,
                )
            else:
                arrived(("y", frame, step))
                part = far_view(frame, area, other_y, my_core, half, rows - half)
                send(("dx", frame, step), part, part, to_x)
                view = far_view(frame, area, other_y, my_core)
                send(("cy", frame, step), view, view, to_core)

    def diagonal(frame):
        for step in range(depth_len):
            arrived(("dy", frame, step))
            arrived(("dx", frame, step))
            view = far_view(frame, area_at(step, other_x), other_y, my_core)
            send(("cd", frame, step), view, view, to_core)

    def frame_ready(frame):
        for step in range(depth_len):
            if step > 0:
                arrived(("cz", frame, step))
                arrived(("cy", frame, step))
            arrived(("cx", frame, step))
            arrived(("cd", frame, step))

    def products(blocks, index, weights, row):
        listed = jnp.concatenate(
            [blocks[index[row, link]] for link in range(index.shape[1])], axis=1
        )
        kernel_row = jnp.concatenate(
            [weights[row, link] for link in range(index.shape[1])], axis=1
        )
        return lax.dot_general(
            listed, kernel_row, (((1,), (1,)), ((), ())), preferred_element_type=jnp.float32
        )

    def euler(step):
        def one_row(row, carry):
            lateral = products(near_frames[step + delay_len], local_idx, near_weight, row)
            distant = products(far_frames[step], far_idx, distant_weight, row)
            state = out[row]
            drive = stimulus[row].astype(jnp.float32)
            state = state + leak[pl.ds(row, 1), :] * (-state + lateral + distant + drive)
            out[row] = state
            if step + 1 < STEPS:
                near_frames[step + delay_len + 1][my_col * rows + row] = softplus(state).astype(
                    jnp.bfloat16
                )
            return carry

        lax.fori_loop(0, rows, one_row, 0)

    own_section(delay_len)
    own_depth(0)
    own_x(0)
    own_section(0)
    column(0)
    for frame in range(1, delay_len):
        own_depth(frame)
        own_x(frame)
        own_section(frame)
    section_arrival(delay_len)
    own_depth(delay_len)
    own_x(delay_len)
    for frame in range(1, delay_len):
        column(frame)
    relay(0)
    diagonal(0)
    for load in loads[delay_len:]:
        load.wait()
    for step in range(STEPS):
        if step > 0:
            relay(step)
            diagonal(step)
        frame = step + delay_len
        if step > 0:
            section_arrival(frame)
        section_ready(frame)
        frame_ready(step)
        euler(step)
        following = frame + 1
        if step + 1 < STEPS:
            own_section(following)
            if following < frame_count:
                own_depth(following)
                own_x(following)
        if frame < frame_count:
            column(frame)
    for copy in started.values():
        copy.wait_send()


def shards_gather(
    initial_state,
    past_rates,
    stimulus,
    leak_rate,
    local_weight,
    far_weight,
    local_index,
    area_sizes,
    far_area,
    far_offset,
):
    area_count = lax.axis_size("area")
    col_count = lax.axis_size("col")
    rows, trials, block_len = initial_state.shape
    first_row = (lax.axis_index("area") * col_count + lax.axis_index("col")) * rows
    delay_len = past_rates.shape[0]
    section_len = rows * col_count
    block_count = section_len * area_count
    my_areas = lax.dynamic_slice_in_dim(far_area, first_row, rows)
    my_offsets = lax.dynamic_slice_in_dim(far_offset, first_row, rows)
    area_len = jnp.zeros_like(my_areas)
    area_first = jnp.zeros_like(my_areas)
    for area in range(area_sizes.shape[0]):
        area_len = area_len + jnp.where(my_areas == area, area_sizes[area], 0)
        area_first = area_first + jnp.where(my_areas > area, area_sizes[area], 0)
    far_block = area_first * section_len + my_offsets % (area_len * section_len)
    depth_len = area_count // PLANE
    copies = copy_count(depth_len, STEPS, delay_len)
    block = (trials, block_len)
    vmem = pl.BlockSpec(memory_space=pltpu.VMEM)
    smem = pl.BlockSpec(memory_space=pltpu.SMEM)
    hbm = pl.BlockSpec(memory_space=pl.ANY)
    links = local_weight.shape[1] + far_weight.shape[1]
    return pl.pallas_call(
        functools.partial(kernel, (depth_len, rows)),
        out_shape=jax.ShapeDtypeStruct(initial_state.shape, jnp.float32),
        in_specs=[smem, smem, vmem, vmem, vmem, hbm, hbm, hbm],
        out_specs=vmem,
        scratch_shapes=[pltpu.VMEM((block_count,) + block, jnp.bfloat16) for _ in range(STEPS)]
        + [pltpu.VMEM((section_len,) + block, jnp.bfloat16) for _ in range(STEPS + delay_len)]
        + [
            pltpu.VMEM(local_weight.shape, jnp.bfloat16),
            pltpu.VMEM(far_weight.shape, jnp.bfloat16),
            pltpu.SemaphoreType.DMA((delay_len + 2,)),
            pltpu.SemaphoreType.DMA((copies,)),
            pltpu.SemaphoreType.DMA((copies,)),
        ],
        compiler_params=pltpu.CompilerParams(
            collective_id=0, has_side_effects=True, vmem_limit_bytes=VMEM_GRANT
        ),
        cost_estimate=pl.CostEstimate(
            flops=2 * STEPS * rows * links * trials * block_len * block_len,
            bytes_accessed=2 * rows * (links + 8) * trials * block_len,
            transcendentals=2 * STEPS * rows * trials * block_len,
        ),
    )(far_block, local_index, initial_state, stimulus, leak_rate, past_rates, local_weight, far_weight)


def copy_count(depth_len, steps, delay_len):
    per_frame = 3 * (depth_len - 1) + 6 * depth_len
    return steps * per_frame + 3 * steps


def shards(*arrays):
    initial_state, past_rates = arrays[0], arrays[1]
    area_count = lax.axis_size("area")
    col_count = lax.axis_size("col")
    shard_bytes = past_rates[0].size * past_rates.dtype.itemsize
    held = STEPS * shard_bytes * area_count * col_count
    held += (STEPS + past_rates.shape[0]) * shard_bytes * col_count
    held += sum(array.size * array.dtype.itemsize for array in arrays[4:6])
    held += 3 * initial_state.size * initial_state.dtype.itemsize
    planar = col_count == CORES * 2 and area_count % PLANE == 0 and initial_state.shape[0] % 2 == 0
    if planar and held < VMEM_GRANT:
        return shards_gather(*arrays)
    return shards_exchange(*arrays)


def solution(mesh):
    return jax.shard_map(
        shards,
        mesh=mesh,
        in_specs=(
            P(("area", "col"), None, None),
            P(None, ("area", "col"), None, None),
            P(("area", "col"), None, None),
            P(("area", "col"), None),
            P(("area", "col"), None, None, None),
            P(("area", "col"), None, None, None),
            P(("area", "col"), None),
            P(),
            P(),
            P(),
        ),
        out_specs=P(("area", "col"), None, None),
        check_vma=False,
    )
```

```python
import functools

import jax
import jax.numpy as jnp
from jax import lax
from jax.sharding import PartitionSpec as P

from jax.experimental import pallas as pl
from jax.experimental.pallas import tpu as pltpu

STEPS = 4
CORES = 2
PLANE = 2
VMEM_GRANT = 60 * 1024 * 1024


def shards_exchange(
    initial_state,
    past_rates,
    stimulus,
    leak_rate,
    local_weight,
    far_weight,
    local_index,
    area_sizes,
    far_area,
    far_offset,
):
    area_count = lax.axis_size("area")
    col_count = lax.axis_size("col")
    my_area = lax.axis_index("area")
    my_col = lax.axis_index("col")
    row_count = initial_state.shape[0]
    trial_count = initial_state.shape[1]
    block_len = initial_state.shape[2]
    link_count = row_count * far_weight.shape[1]
    slot_count = 2 * link_count // area_count
    section_len = row_count * col_count
    delay_len = past_rates.shape[0]
    area_ids = jnp.arange(area_sizes.shape[0], dtype=jnp.int32)
    starts = jnp.cumsum(area_sizes) - area_sizes
    match_area = far_area[..., None] == area_ids
    area_len = jnp.sum(jnp.where(match_area, area_sizes, 0), axis=-1)
    area_first = jnp.sum(jnp.where(match_area, starts, 0), axis=-1)
    far_block = area_first * section_len + far_offset % (area_len * section_len)
    by_device = far_block.reshape(area_count, col_count, link_count)
    same_col = lax.dynamic_index_in_dim(by_device, my_col, axis=1, keepdims=False)
    section_of = same_col // section_len
    placing = same_col % section_len
    earlier = jnp.tril(jnp.ones((link_count, link_count), jnp.bool_), -1)
    order_rank = jnp.sum(
        (section_of[:, :, None] == section_of[:, None, :]) & earlier[None], axis=-1
    )
    slot_ids = jnp.arange(slot_count, dtype=order_rank.dtype)
    wanted = (section_of[:, None, :] == my_area) & (
        order_rank[:, None, :] == slot_ids[None, :, None]
    )
    slot_place = jnp.sum(jnp.where(wanted, placing[:, None, :], 0), axis=-1).reshape(-1)
    slot_used = jnp.any(wanted, axis=-1).reshape(-1)
    own_section = lax.dynamic_index_in_dim(section_of, my_area, axis=0, keepdims=False)
    own_rank = lax.dynamic_index_in_dim(order_rank, my_area, axis=0, keepdims=False)
    arrival = own_section * slot_count + own_rank
    leak_gain = leak_rate[:, None, :]
    drive_term = stimulus.astype(jnp.float32)
    membrane = initial_state
    rate_now = jax.nn.softplus(membrane).astype(jnp.bfloat16)
    sections = []
    for step_idx in range(STEPS):
        section = lax.all_gather(rate_now, "col", axis=0, tiled=True)
        sections.append(section)
        if step_idx < delay_len:
            source = lax.all_gather(past_rates[step_idx], "col", axis=0, tiled=True)
        else:
            source = sections[step_idx - delay_len]
        frames = source[None]
        picked = frames[:, slot_place]
        arrived = lax.all_to_all(
            jnp.where(slot_used[None, :, None, None], picked, jnp.zeros((), frames.dtype)),
            "area",
            split_axis=1,
            concat_axis=1,
            tiled=True,
        )[0]
        lateral = jnp.einsum(
            "rktb,rkob->rto", section[local_index], local_weight, preferred_element_type=jnp.float32
        )
        distant = jnp.einsum(
            "rktb,rkob->rto",
            arrived[arrival].reshape(row_count, -1, trial_count, block_len),
            far_weight,
            preferred_element_type=jnp.float32,
        )
        membrane = membrane + leak_gain * (-membrane + lateral + distant + drive_term)
        if step_idx + 1 < STEPS:
            rate_now = jax.nn.softplus(membrane).astype(jnp.bfloat16)
    return membrane


def softplus(values):
    return jnp.maximum(values, 0.0) + jnp.log1p(jnp.exp(-jnp.abs(values)))


def kernel(
    dims,
    far_idx,
    local_idx,
    initial,
    stimulus,
    leak,
    past,
    local_weight,
    far_weight,
    out,
    *scratch,
):
    depth_len, rows = dims
    delay_len = past.shape[0]
    frame_count = STEPS
    far_frames = scratch[:frame_count]
    near_frames = scratch[frame_count : 2 * frame_count + delay_len]
    near_weight, distant_weight, lateral_sum, load_sem, send_sem, recv_sem = scratch[
        2 * frame_count + delay_len :
    ]
    my_area = lax.axis_index("area")
    my_col = lax.axis_index("col")
    my_depth, my_x = my_area // PLANE, my_area % PLANE
    my_y, my_core = my_col // CORES, my_col % CORES
    other_x, other_y, other_core = 1 - my_x, 1 - my_y, 1 - my_core
    col_count = lax.axis_size("col")
    half = rows // 2
    carried = max(1, rows // 8)
    direct = rows - carried

    def paired(step):
        depth, bit = my_depth, 1
        while bit <= step:
            if step // bit % 2:
                depth = depth + bit - 2 * bit * ((depth // bit) % 2)
            bit *= 2
        return depth

    def area_at(step, x_pos):
        return paired(step) * PLANE + x_pos

    to_x = {"area": my_depth * PLANE + other_x, "col": my_col}
    to_y = {"area": my_area, "col": other_y * CORES + my_core}
    to_core = {"area": my_area, "col": my_y * CORES + other_core}

    def to_depth(step):
        return {"area": area_at(step, my_x), "col": my_col}

    partners = [to_depth(step) for step in range(1, depth_len)] + [to_x, to_y, to_core]

    loads = [
        pltpu.make_async_copy(
            past.at[index], near_frames[index].at[pl.ds(my_col * rows, rows)], load_sem.at[index]
        )
        for index in range(delay_len)
    ]
    loads.append(pltpu.make_async_copy(local_weight, near_weight, load_sem.at[delay_len]))
    loads.append(pltpu.make_async_copy(far_weight, distant_weight, load_sem.at[delay_len + 1]))
    for load in loads:
        load.start()

    barrier = pltpu.get_barrier_semaphore()
    for partner in partners:
        pl.semaphore_signal(barrier, inc=1, device_id=partner, device_id_type=pl.DeviceIdType.MESH)

    pl.semaphore_wait(barrier, len(partners))
    for load in loads[:delay_len]:
        load.wait()

    def prepare(row, carry):
        state = initial[row]
        out[row] = state
        near_frames[delay_len][my_col * rows + row] = softplus(state).astype(jnp.bfloat16)
        return carry

    started = {}
    numbers = {}

    def near_view(frame, y_pos, core, first=0, count=None):
        start = (y_pos * CORES + core) * rows + first
        return near_frames[frame].at[pl.ds(start, rows if count is None else count)]

    def far_view(frame, area, y_pos, core, first=0, count=None):
        start = (area * col_count + y_pos * CORES + core) * rows + first
        return far_frames[frame].at[pl.ds(start, rows if count is None else count)]

    def send(key, source, target, device):
        number = numbers.setdefault(key, len(numbers))
        copy = pltpu.make_async_remote_copy(
            src_ref=source,
            dst_ref=target,
            send_sem=send_sem.at[number],
            recv_sem=recv_sem.at[number],
            device_id=device,
            device_id_type=pl.DeviceIdType.MESH,
        )
        copy.start()
        started[key] = copy

    def arrived(key):
        started[key].wait_recv()

    def own_depth(frame):
        mine = near_view(frame, my_y, my_core)
        for step in range(1, depth_len):
            send(("z", frame, step), mine, far_view(frame, my_area, my_y, my_core), to_depth(step))

    def own_x(frame):
        mine = near_view(frame, my_y, my_core)
        send(("x", frame, 0), mine, far_view(frame, my_area, my_y, my_core), to_x)

    def own_section(frame):
        if frame < delay_len:
            part = near_view(frame, my_y, my_core, half, rows - half)
            send(("y", frame, 0), part, part, to_y)
        else:
            mine = near_view(frame, my_y, my_core)
            send(("y", frame, 0), mine, mine, to_y)
            send(("c", frame), mine, mine, to_core)

    def column(frame, step):
        arrived(("z", frame, step))
        view = far_view(frame, area_at(step, my_x), my_y, my_core)
        part = far_view(frame, area_at(step, my_x), my_y, my_core, 0, direct)
        send(("x", frame, step), part, part, to_x)
        send(("y", frame, step), part, part, to_y)
        send(("cz", frame, step), view, view, to_core)

    def section_arrival(frame):
        arrived(("y", frame, 0))
        view = near_view(frame, other_y, my_core)
        send(("cy", frame, 0), view, view, to_core)

    def section_ready(frame):
        arrived(("c", frame))
        arrived(("cy", frame, 0))

    def relay(frame, step):
        arrived(("x", frame, step))
        area = area_at(step, other_x)
        part = far_view(frame, area, my_y, my_core, 0, half)
        send(("dy", frame, step), part, part, to_y)
        if step > 0:
            arrived(("zx", frame, step))
        view = far_view(frame, area, my_y, my_core)
        send(("cx", frame, step), view, view, to_core)
        area = area_at(step, my_x)
        if step == 0:
            if frame < delay_len:
                arrived(("y", frame, 0))
            part = near_view(frame, other_y, my_core, half, rows - half)
            send(
                ("dx", frame, step),
                part,
                far_view(frame, area, other_y, my_core, half, rows - half),
                to_x,
            )
            for other in range(1, depth_len):
                part = far_view(frame, my_depth * PLANE + other_x, my_y, my_core, direct, carried)
                send(("zx", frame, other), part, part, to_depth(other))
                part = near_view(frame, other_y, my_core, direct, carried)
                target = far_view(frame, my_area, other_y, my_core, direct, carried)
                send(("zy", frame, other), part, target, to_depth(other))
        else:
            arrived(("y", frame, step))
            arrived(("zy", frame, step))
            part = far_view(frame, area, other_y, my_core, half, rows - half)
            send(("dx", frame, step), part, part, to_x)
            view = far_view(frame, area, other_y, my_core)
            send(("cy", frame, step), view, view, to_core)

    def diagonal(frame, step):
        arrived(("dy", frame, step))
        arrived(("dx", frame, step))
        view = far_view(frame, area_at(step, other_x), other_y, my_core)
        send(("cd", frame, step), view, view, to_core)

    def frame_ready(frame):
        for step in range(depth_len):
            if step > 0:
                arrived(("cz", frame, step))
                arrived(("cy", frame, step))
            arrived(("cx", frame, step))
            arrived(("cd", frame, step))

    def products(blocks, index, weights, row):
        listed = jnp.concatenate(
            [blocks[index[row, link]] for link in range(index.shape[1])], axis=1
        )
        kernel_row = jnp.concatenate(
            [weights[row, link] for link in range(index.shape[1])], axis=1
        )
        return lax.dot_general(
            listed, kernel_row, (((1,), (1,)), ((), ())), preferred_element_type=jnp.float32
        )

    def add_lateral(step):
        def one_row(row, carry):
            lateral_sum[row] = products(near_frames[step + delay_len], local_idx, near_weight, row)
            return carry

        lax.fori_loop(0, rows, one_row, 0)

    def euler(step):
        def one_row(row, carry):
            distant = products(far_frames[step], far_idx, distant_weight, row)
            state = out[row]
            drive = stimulus[row].astype(jnp.float32)
            change = -state + lateral_sum[row] + distant + drive
            state = state + leak[pl.ds(row, 1), :] * change
            out[row] = state
            if step + 1 < STEPS:
                near_frames[step + delay_len + 1][my_col * rows + row] = softplus(state).astype(
                    jnp.bfloat16
                )
            return carry

        lax.fori_loop(0, rows, one_row, 0)

    steps = range(1, depth_len)
    own_depth(0)
    for frame in range(delay_len):
        own_x(frame)
        own_section(frame)
    lax.fori_loop(0, rows, prepare, 0)
    own_section(delay_len)
    own_x(delay_len)
    column(0, 1)
    relay(0, 0)
    for step in range(2, depth_len):
        column(0, step)
    own_depth(1)
    section_arrival(delay_len)
    for frame in (*range(1, delay_len), delay_len):
        relay(frame, 0)
    for step in range(STEPS):
        frame = step + delay_len
        if step == 0:
            for load in loads[delay_len:]:
                load.wait()
        for part in steps:
            if step + 1 < frame_count:
                column(step + 1, part)
            if step == 0 and part + 1 == depth_len:
                own_depth(delay_len)
            relay(step, part)
        if step > 0:
            section_arrival(frame)
            if delay_len < frame < frame_count:
                relay(frame, 0)
        section_ready(frame)
        add_lateral(step)
        for part in range(depth_len):
            diagonal(step, part)
        frame_ready(step)
        euler(step)
        if step + 1 < STEPS:
            own_section(frame + 1)
            if frame + 1 < frame_count:
                own_depth(frame + 1)
                own_x(frame + 1)
    for copy in started.values():
        copy.wait_send()


def shards_gather(
    initial_state,
    past_rates,
    stimulus,
    leak_rate,
    local_weight,
    far_weight,
    local_index,
    area_sizes,
    far_area,
    far_offset,
):
    area_count = lax.axis_size("area")
    col_count = lax.axis_size("col")
    rows, trials, block_len = initial_state.shape
    first_row = (lax.axis_index("area") * col_count + lax.axis_index("col")) * rows
    delay_len = past_rates.shape[0]
    section_len = rows * col_count
    block_count = section_len * area_count
    my_areas = lax.dynamic_slice_in_dim(far_area, first_row, rows)
    my_offsets = lax.dynamic_slice_in_dim(far_offset, first_row, rows)
    area_len = jnp.zeros_like(my_areas)
    area_first = jnp.zeros_like(my_areas)
    for area in range(area_sizes.shape[0]):
        area_len = area_len + jnp.where(my_areas == area, area_sizes[area], 0)
        area_first = area_first + jnp.where(my_areas > area, area_sizes[area], 0)
    span = area_len * section_len
    turns = (my_offsets.astype(jnp.float32) / span.astype(jnp.float32)).astype(jnp.int32)
    place = my_offsets - turns * span
    place = jnp.where(place < 0, place + span, jnp.where(place >= span, place - span, place))
    far_block = area_first * section_len + place
    depth_len = area_count // PLANE
    copies = copy_count(depth_len, STEPS, delay_len)
    block = (trials, block_len)
    vmem = pl.BlockSpec(memory_space=pltpu.VMEM)
    smem = pl.BlockSpec(memory_space=pltpu.SMEM)
    hbm = pl.BlockSpec(memory_space=pl.ANY)
    links = local_weight.shape[1] + far_weight.shape[1]
    return pl.pallas_call(
        functools.partial(kernel, (depth_len, rows)),
        out_shape=jax.ShapeDtypeStruct(initial_state.shape, jnp.float32),
        in_specs=[smem, smem, vmem, vmem, vmem, hbm, hbm, hbm],
        out_specs=vmem,
        scratch_shapes=[pltpu.VMEM((block_count,) + block, jnp.bfloat16) for _ in range(STEPS)]
        + [pltpu.VMEM((section_len,) + block, jnp.bfloat16) for _ in range(STEPS + delay_len)]
        + [
            pltpu.VMEM(local_weight.shape, jnp.bfloat16),
            pltpu.VMEM(far_weight.shape, jnp.bfloat16),
            pltpu.VMEM(initial_state.shape, jnp.float32),
            pltpu.SemaphoreType.DMA((delay_len + 2,)),
            pltpu.SemaphoreType.DMA((copies,)),
            pltpu.SemaphoreType.DMA((copies,)),
        ],
        compiler_params=pltpu.CompilerParams(
            collective_id=0, has_side_effects=True, vmem_limit_bytes=VMEM_GRANT
        ),
        cost_estimate=pl.CostEstimate(
            flops=2 * STEPS * rows * links * trials * block_len * block_len,
            bytes_accessed=2 * rows * (links + 8) * trials * block_len,
            transcendentals=2 * STEPS * rows * trials * block_len,
        ),
    )(
        far_block,
        local_index,
        initial_state,
        stimulus,
        leak_rate,
        past_rates,
        local_weight,
        far_weight,
    )


def copy_count(depth_len, steps, delay_len):
    per_frame = 5 * (depth_len - 1) + 6 * depth_len
    return steps * per_frame + 3 * steps


def shards(*arrays):
    initial_state, past_rates = arrays[0], arrays[1]
    area_count = lax.axis_size("area")
    col_count = lax.axis_size("col")
    shard_bytes = past_rates[0].size * past_rates.dtype.itemsize
    held = STEPS * shard_bytes * area_count * col_count
    held += (STEPS + past_rates.shape[0]) * shard_bytes * col_count
    held += sum(array.size * array.dtype.itemsize for array in arrays[4:6])
    held += 3 * initial_state.size * initial_state.dtype.itemsize
    planar = col_count == CORES * 2 and area_count % PLANE == 0 and initial_state.shape[0] % 2 == 0
    depth_len = area_count // PLANE
    planar = planar and depth_len & (depth_len - 1) == 0
    if planar and held < VMEM_GRANT:
        return shards_gather(*arrays)
    return shards_exchange(*arrays)


def solution(mesh):
    return jax.shard_map(
        shards,
        mesh=mesh,
        in_specs=(
            P(("area", "col"), None, None),
            P(None, ("area", "col"), None, None),
            P(("area", "col"), None, None),
            P(("area", "col"), None),
            P(("area", "col"), None, None, None),
            P(("area", "col"), None, None, None),
            P(("area", "col"), None),
            P(),
            P(),
            P(),
        ),
        out_specs=P(("area", "col"), None, None),
        check_vma=False,
    )
```

```python
import functools

import jax
import jax.numpy as jnp
from jax import lax
from jax.sharding import PartitionSpec as P

from jax.experimental import pallas as pl
from jax.experimental.pallas import tpu as pltpu

STEPS = 4
CORES = 2
PLANE = 2
VMEM_GRANT = 60 * 1024 * 1024


def shards_exchange(
    initial_state,
    past_rates,
    stimulus,
    leak_rate,
    local_weight,
    far_weight,
    local_index,
    area_sizes,
    far_area,
    far_offset,
):
    area_count = lax.axis_size("area")
    col_count = lax.axis_size("col")
    my_area = lax.axis_index("area")
    my_col = lax.axis_index("col")
    row_count = initial_state.shape[0]
    trial_count = initial_state.shape[1]
    block_len = initial_state.shape[2]
    link_count = row_count * far_weight.shape[1]
    slot_count = 2 * link_count // area_count
    section_len = row_count * col_count
    delay_len = past_rates.shape[0]
    area_ids = jnp.arange(area_sizes.shape[0], dtype=jnp.int32)
    starts = jnp.cumsum(area_sizes) - area_sizes
    match_area = far_area[..., None] == area_ids
    area_len = jnp.sum(jnp.where(match_area, area_sizes, 0), axis=-1)
    area_first = jnp.sum(jnp.where(match_area, starts, 0), axis=-1)
    far_block = area_first * section_len + far_offset % (area_len * section_len)
    by_device = far_block.reshape(area_count, col_count, link_count)
    same_col = lax.dynamic_index_in_dim(by_device, my_col, axis=1, keepdims=False)
    section_of = same_col // section_len
    placing = same_col % section_len
    earlier = jnp.tril(jnp.ones((link_count, link_count), jnp.bool_), -1)
    order_rank = jnp.sum(
        (section_of[:, :, None] == section_of[:, None, :]) & earlier[None], axis=-1
    )
    slot_ids = jnp.arange(slot_count, dtype=order_rank.dtype)
    wanted = (section_of[:, None, :] == my_area) & (
        order_rank[:, None, :] == slot_ids[None, :, None]
    )
    slot_place = jnp.sum(jnp.where(wanted, placing[:, None, :], 0), axis=-1).reshape(-1)
    slot_used = jnp.any(wanted, axis=-1).reshape(-1)
    own_section = lax.dynamic_index_in_dim(section_of, my_area, axis=0, keepdims=False)
    own_rank = lax.dynamic_index_in_dim(order_rank, my_area, axis=0, keepdims=False)
    arrival = own_section * slot_count + own_rank
    leak_gain = leak_rate[:, None, :]
    drive_term = stimulus.astype(jnp.float32)
    membrane = initial_state
    rate_now = jax.nn.softplus(membrane).astype(jnp.bfloat16)
    sections = []
    for step_idx in range(STEPS):
        section = lax.all_gather(rate_now, "col", axis=0, tiled=True)
        sections.append(section)
        if step_idx < delay_len:
            source = lax.all_gather(past_rates[step_idx], "col", axis=0, tiled=True)
        else:
            source = sections[step_idx - delay_len]
        frames = source[None]
        picked = frames[:, slot_place]
        arrived = lax.all_to_all(
            jnp.where(slot_used[None, :, None, None], picked, jnp.zeros((), frames.dtype)),
            "area",
            split_axis=1,
            concat_axis=1,
            tiled=True,
        )[0]
        lateral = jnp.einsum(
            "rktb,rkob->rto", section[local_index], local_weight, preferred_element_type=jnp.float32
        )
        distant = jnp.einsum(
            "rktb,rkob->rto",
            arrived[arrival].reshape(row_count, -1, trial_count, block_len),
            far_weight,
            preferred_element_type=jnp.float32,
        )
        membrane = membrane + leak_gain * (-membrane + lateral + distant + drive_term)
        if step_idx + 1 < STEPS:
            rate_now = jax.nn.softplus(membrane).astype(jnp.bfloat16)
    return membrane


def softplus(values):
    return jnp.maximum(values, 0.0) + jnp.log1p(jnp.exp(-jnp.abs(values)))


def kernel(
    dims,
    far_idx,
    local_idx,
    initial,
    stimulus,
    leak,
    past,
    local_weight,
    far_weight,
    out,
    *scratch,
):
    depth_len, rows = dims
    delay_len = past.shape[0]
    frame_count = STEPS
    far_frames = scratch[:frame_count]
    near_frames = scratch[frame_count : 2 * frame_count + delay_len]
    near_weight, distant_weight, lateral_sum, load_sem, send_sem, recv_sem = scratch[
        2 * frame_count + delay_len :
    ]
    my_area = lax.axis_index("area")
    my_col = lax.axis_index("col")
    my_depth, my_x = my_area // PLANE, my_area % PLANE
    my_y, my_core = my_col // CORES, my_col % CORES
    other_x, other_y, other_core = 1 - my_x, 1 - my_y, 1 - my_core
    col_count = lax.axis_size("col")
    half = rows // 2
    carried = max(1, rows // 8)
    direct = rows - carried

    def paired(step):
        depth, bit = my_depth, 1
        while bit <= step:
            if step // bit % 2:
                depth = depth + bit - 2 * bit * ((depth // bit) % 2)
            bit *= 2
        return depth

    def area_at(step, x_pos):
        return paired(step) * PLANE + x_pos

    to_x = {"area": my_depth * PLANE + other_x, "col": my_col}
    to_y = {"area": my_area, "col": other_y * CORES + my_core}
    to_core = {"area": my_area, "col": my_y * CORES + other_core}

    def to_depth(step):
        return {"area": area_at(step, my_x), "col": my_col}

    partners = [to_depth(step) for step in range(1, depth_len)] + [to_x, to_y, to_core]

    loads = [
        pltpu.make_async_copy(
            past.at[index], near_frames[index].at[pl.ds(my_col * rows, rows)], load_sem.at[index]
        )
        for index in range(delay_len)
    ]
    loads.append(pltpu.make_async_copy(local_weight, near_weight, load_sem.at[delay_len]))
    loads.append(pltpu.make_async_copy(far_weight, distant_weight, load_sem.at[delay_len + 1]))
    for load in loads:
        load.start()

    barrier = pltpu.get_barrier_semaphore()
    for partner in partners:
        pl.semaphore_signal(barrier, inc=1, device_id=partner, device_id_type=pl.DeviceIdType.MESH)

    pl.semaphore_wait(barrier, len(partners))
    for load in loads[:delay_len]:
        load.wait()

    def prepare(row, carry):
        state = initial[row]
        out[row] = state
        near_frames[delay_len][my_col * rows + row] = softplus(state).astype(jnp.bfloat16)
        return carry

    started = {}
    numbers = {}

    def near_view(frame, y_pos, core, first=0, count=None):
        start = (y_pos * CORES + core) * rows + first
        return near_frames[frame].at[pl.ds(start, rows if count is None else count)]

    def far_view(frame, area, y_pos, core, first=0, count=None):
        start = (area * col_count + y_pos * CORES + core) * rows + first
        return far_frames[frame].at[pl.ds(start, rows if count is None else count)]

    def send(key, source, target, device):
        number = numbers.setdefault(key, len(numbers))
        copy = pltpu.make_async_remote_copy(
            src_ref=source,
            dst_ref=target,
            send_sem=send_sem.at[number],
            recv_sem=recv_sem.at[number],
            device_id=device,
            device_id_type=pl.DeviceIdType.MESH,
        )
        copy.start()
        started[key] = copy

    def arrived(key):
        started[key].wait_recv()

    def own_depth(frame):
        mine = near_view(frame, my_y, my_core)
        for step in range(1, depth_len):
            send(("z", frame, step), mine, far_view(frame, my_area, my_y, my_core), to_depth(step))

    def own_x(frame):
        mine = near_view(frame, my_y, my_core)
        send(("x", frame, 0), mine, far_view(frame, my_area, my_y, my_core), to_x)

    def own_section(frame):
        if frame < delay_len:
            part = near_view(frame, my_y, my_core, half, rows - half)
            send(("y", frame, 0), part, part, to_y)
        else:
            mine = near_view(frame, my_y, my_core)
            send(("y", frame, 0), mine, mine, to_y)
            send(("c", frame), mine, mine, to_core)

    def column(frame, step):
        arrived(("z", frame, step))
        view = far_view(frame, area_at(step, my_x), my_y, my_core)
        part = far_view(frame, area_at(step, my_x), my_y, my_core, 0, direct)
        send(("x", frame, step), part, part, to_x)
        send(("y", frame, step), part, part, to_y)
        send(("cz", frame, step), view, view, to_core)

    def section_arrival(frame):
        arrived(("y", frame, 0))
        view = near_view(frame, other_y, my_core)
        send(("cy", frame, 0), view, view, to_core)

    def section_ready(frame):
        arrived(("c", frame))
        arrived(("cy", frame, 0))

    def relay(frame, step):
        arrived(("x", frame, step))
        area = area_at(step, other_x)
        part = far_view(frame, area, my_y, my_core, 0, half)
        send(("dy", frame, step), part, part, to_y)
        if step > 0:
            arrived(("zx", frame, step))
        view = far_view(frame, area, my_y, my_core)
        send(("cx", frame, step), view, view, to_core)
        area = area_at(step, my_x)
        if step == 0:
            if frame < delay_len:
                arrived(("y", frame, 0))
            part = near_view(frame, other_y, my_core, half, rows - half)
            send(
                ("dx", frame, step),
                part,
                far_view(frame, area, other_y, my_core, half, rows - half),
                to_x,
            )
            for other in range(1, depth_len):
                part = far_view(frame, my_depth * PLANE + other_x, my_y, my_core, direct, carried)
                send(("zx", frame, other), part, part, to_depth(other))
                part = near_view(frame, other_y, my_core, direct, carried)
                target = far_view(frame, my_area, other_y, my_core, direct, carried)
                send(("zy", frame, other), part, target, to_depth(other))
        else:
            arrived(("y", frame, step))
            arrived(("zy", frame, step))
            part = far_view(frame, area, other_y, my_core, half, rows - half)
            send(("dx", frame, step), part, part, to_x)
            view = far_view(frame, area, other_y, my_core)
            send(("cy", frame, step), view, view, to_core)

    def diagonal(frame, step):
        arrived(("dy", frame, step))
        arrived(("dx", frame, step))
        view = far_view(frame, area_at(step, other_x), other_y, my_core)
        send(("cd", frame, step), view, view, to_core)

    def frame_ready(frame):
        for step in range(depth_len):
            if step > 0:
                arrived(("cz", frame, step))
                arrived(("cy", frame, step))
            arrived(("cx", frame, step))
            arrived(("cd", frame, step))

    def products(blocks, index, weights, row):
        listed = jnp.concatenate(
            [blocks[index[row, link]] for link in range(index.shape[1])], axis=1
        )
        kernel_row = jnp.concatenate(
            [weights[row, link] for link in range(index.shape[1])], axis=1
        )
        return lax.dot_general(
            listed, kernel_row, (((1,), (1,)), ((), ())), preferred_element_type=jnp.float32
        )

    def add_lateral(step):
        def one_row(row, carry):
            lateral_sum[row] = products(near_frames[step + delay_len], local_idx, near_weight, row)
            return carry

        lax.fori_loop(0, rows, one_row, 0)

    def euler(step):
        def one_row(row, carry):
            distant = products(far_frames[step], far_idx, distant_weight, row)
            state = out[row]
            drive = stimulus[row].astype(jnp.float32)
            change = -state + lateral_sum[row] + distant + drive
            state = state + leak[pl.ds(row, 1), :] * change
            out[row] = state
            if step + 1 < STEPS:
                near_frames[step + delay_len + 1][my_col * rows + row] = softplus(state).astype(
                    jnp.bfloat16
                )
            return carry

        lax.fori_loop(0, rows, one_row, 0)

    issued = set()

    def once(action, frame, part):
        if (action, frame, part) not in issued:
            issued.add((action, frame, part))
            action(frame, part)

    steps = range(1, depth_len)
    own_depth(0)
    for frame in range(delay_len):
        own_x(frame)
        own_section(frame)
    lax.fori_loop(0, rows, prepare, 0)
    own_section(delay_len)
    own_x(delay_len)
    column(0, 1)
    relay(0, 0)
    for step in range(2, depth_len):
        column(0, step)
    own_depth(1)
    section_arrival(delay_len)
    for frame in (*range(1, delay_len), delay_len):
        relay(frame, 0)
    for step in range(STEPS):
        frame = step + delay_len
        if step == 0:
            for load in loads[delay_len:]:
                load.wait()
        for part in steps:
            once(relay, step, part)
            if step + 1 < frame_count:
                once(column, step + 1, part)
            if step == 0 and part == 1:
                own_depth(delay_len)
        if step > 0:
            section_arrival(frame)
            if delay_len < frame < frame_count:
                relay(frame, 0)
        section_ready(frame)
        if step + 2 < frame_count:
            for part in steps[:-1]:
                once(column, step + 2, part)
        if step + 1 < frame_count:
            once(relay, step + 1, 1)
        add_lateral(step)
        for part in range(depth_len):
            diagonal(step, part)
        frame_ready(step)
        euler(step)
        if step + 1 < STEPS:
            own_section(frame + 1)
            if frame + 1 < frame_count:
                own_depth(frame + 1)
                own_x(frame + 1)
    for copy in started.values():
        copy.wait_send()


def shards_gather(
    initial_state,
    past_rates,
    stimulus,
    leak_rate,
    local_weight,
    far_weight,
    local_index,
    area_sizes,
    far_area,
    far_offset,
):
    area_count = lax.axis_size("area")
    col_count = lax.axis_size("col")
    rows, trials, block_len = initial_state.shape
    first_row = (lax.axis_index("area") * col_count + lax.axis_index("col")) * rows
    delay_len = past_rates.shape[0]
    section_len = rows * col_count
    block_count = section_len * area_count
    my_areas = lax.dynamic_slice_in_dim(far_area, first_row, rows)
    my_offsets = lax.dynamic_slice_in_dim(far_offset, first_row, rows)
    area_len = jnp.zeros_like(my_areas)
    area_first = jnp.zeros_like(my_areas)
    for area in range(area_sizes.shape[0]):
        area_len = area_len + jnp.where(my_areas == area, area_sizes[area], 0)
        area_first = area_first + jnp.where(my_areas > area, area_sizes[area], 0)
    span = area_len * section_len
    turns = (my_offsets.astype(jnp.float32) / span.astype(jnp.float32)).astype(jnp.int32)
    place = my_offsets - turns * span
    place = jnp.where(place < 0, place + span, jnp.where(place >= span, place - span, place))
    far_block = area_first * section_len + place
    depth_len = area_count // PLANE
    copies = copy_count(depth_len, STEPS, delay_len)
    block = (trials, block_len)
    vmem = pl.BlockSpec(memory_space=pltpu.VMEM)
    smem = pl.BlockSpec(memory_space=pltpu.SMEM)
    hbm = pl.BlockSpec(memory_space=pl.ANY)
    links = local_weight.shape[1] + far_weight.shape[1]
    return pl.pallas_call(
        functools.partial(kernel, (depth_len, rows)),
        out_shape=jax.ShapeDtypeStruct(initial_state.shape, jnp.float32),
        in_specs=[smem, smem, vmem, vmem, vmem, hbm, hbm, hbm],
        out_specs=vmem,
        scratch_shapes=[pltpu.VMEM((block_count,) + block, jnp.bfloat16) for _ in range(STEPS)]
        + [pltpu.VMEM((section_len,) + block, jnp.bfloat16) for _ in range(STEPS + delay_len)]
        + [
            pltpu.VMEM(local_weight.shape, jnp.bfloat16),
            pltpu.VMEM(far_weight.shape, jnp.bfloat16),
            pltpu.VMEM(initial_state.shape, jnp.float32),
            pltpu.SemaphoreType.DMA((delay_len + 2,)),
            pltpu.SemaphoreType.DMA((copies,)),
            pltpu.SemaphoreType.DMA((copies,)),
        ],
        compiler_params=pltpu.CompilerParams(
            collective_id=0, has_side_effects=True, vmem_limit_bytes=VMEM_GRANT
        ),
        cost_estimate=pl.CostEstimate(
            flops=2 * STEPS * rows * links * trials * block_len * block_len,
            bytes_accessed=2 * rows * (links + 8) * trials * block_len,
            transcendentals=2 * STEPS * rows * trials * block_len,
        ),
    )(
        far_block,
        local_index,
        initial_state,
        stimulus,
        leak_rate,
        past_rates,
        local_weight,
        far_weight,
    )


def copy_count(depth_len, steps, delay_len):
    per_frame = 5 * (depth_len - 1) + 6 * depth_len
    return steps * per_frame + 3 * steps


def shards(*arrays):
    initial_state, past_rates = arrays[0], arrays[1]
    area_count = lax.axis_size("area")
    col_count = lax.axis_size("col")
    shard_bytes = past_rates[0].size * past_rates.dtype.itemsize
    held = STEPS * shard_bytes * area_count * col_count
    held += (STEPS + past_rates.shape[0]) * shard_bytes * col_count
    held += sum(array.size * array.dtype.itemsize for array in arrays[4:6])
    held += 3 * initial_state.size * initial_state.dtype.itemsize
    planar = col_count == CORES * 2 and area_count % PLANE == 0 and initial_state.shape[0] % 2 == 0
    depth_len = area_count // PLANE
    planar = planar and depth_len & (depth_len - 1) == 0
    if planar and held < VMEM_GRANT:
        return shards_gather(*arrays)
    return shards_exchange(*arrays)


def solution(mesh):
    return jax.shard_map(
        shards,
        mesh=mesh,
        in_specs=(
            P(("area", "col"), None, None),
            P(None, ("area", "col"), None, None),
            P(("area", "col"), None, None),
            P(("area", "col"), None),
            P(("area", "col"), None, None, None),
            P(("area", "col"), None, None, None),
            P(("area", "col"), None),
            P(),
            P(),
            P(),
        ),
        out_specs=P(("area", "col"), None, None),
        check_vma=False,
    )
```
